512 devices in a mesh: leaf: 16 (over y, core), row: 8 (over z), col: 4 (over x).
Axes of the slice: x: 4, y: 8, z: 8, core: 2. Of those that a mesh axis runs over, the one named last changes fastest.
Arguments:
- rhs_leafs: bfloat16 [16384, 256], P(('leaf', 'row', 'col')), may hold values from -6 to 6
- rhs_mid: bfloat16 [16384, 256], P(('leaf', 'row', 'col')), may hold values from -6 to 6
- rhs_root: bfloat16 [16384, 256], P(('leaf', 'row', 'col')), may hold values from -6 to 6
- inv_leafs: bfloat16 [16384, 32, 128], P('leaf', ('row', 'col')), may hold values from -0.09375 to 0.09375
- inv_mid: bfloat16 [16384, 32, 256], P('leaf', ('row', 'col')), may hold values from -0.0625 to 0.0625
- inv_root: bfloat16 [16384, 32, 512], P('leaf', ('row', 'col')), may hold values from -0.046875 to 0.046875
- off_leafs: bfloat16 [8192, 32, 128], P('leaf', ('row', 'col')), may hold values from -0.09375 to 0.09375
- off_mid: bfloat16 [8192, 32, 256], P('leaf', ('row', 'col')), may hold values from -0.0625 to 0.0625
- owner_leafs: int32 [8192, 1], P('leaf'), may hold values from 0 to 31; in each aligned block of 512 rows (0 to 511, 512 to 1023, ...) at most 32 rows name the same one
- offset_leafs: int32 [8192], P('leaf'), may hold values from 0 to 63
- owner_mid: int32 [8192, 1], P('leaf'), may hold values from 0 to 31; in each aligned block of 512 rows (0 to 511, 512 to 1023, ...) at most 32 rows name the same one
- offset_mid: int32 [8192], P('leaf'), may hold values from 0 to 31
Outputs:
- solution_leafs: bfloat16 [16384, 256], P(('leaf', 'row', 'col'))
- solution_mid: bfloat16 [16384, 256], P(('leaf', 'row', 'col'))
- solution_root: bfloat16 [16384, 256], P(('leaf', 'row', 'col'))
The draws below stay inside these ranges and needn't reach their ends.
Inputs may be any that keep to these rules, and one draw needn't show every extreme that they name: `owner_leafs`: in each leaf group's block of 512 rows no device is named more than 32 times, and some device is named exactly 32 times. `owner_mid`: in each leaf group's block of 512 rows no device is named more than 32 times, and some device is named exactly 32 times.
All inputs are finite; a program needn't handle non-finite values.
Results may differ from the reference program's by a relative error of at most 0.033.
Values may be sent and summed in bfloat16 or wider, within the bound.
A program may use at most 64 MiB of HBM per device.

```python
import math
import jax
import jax.numpy as jnp
import numpy as np
from jax import lax

ROWS_DEV = 32
NRHS = 256
OFF_LEAF = 512
CAP = 32
TOTAL = 16384
W_ROOT = 16384
W_MID = 8192
W_LEAF = 4096
N_LEAF = 16
N_ROW = 8
N_COL = 4


def touch_ends(drawn, stream_key, smallest, high):
    longest = drawn.shape.index(max(drawn.shape))
    spots = []
    for shift in (0, 1):
        where = [jax.random.randint(jax.random.fold_in(stream_key, axis), (), 0, length) for axis, length in enumerate(drawn.shape)]
        where[longest] = (where[longest] + shift) % drawn.shape[longest]
        spots.append(tuple(where))
    return drawn.at[spots[0]].set(smallest).at[spots[1]].set(high)


def block_levels(own_key, dims, shards, smallest, top_value):
    level, own = 1.0, jax.random.fold_in(own_key, 6)
    for position, parts in shards:
        heights = jnp.exp(jax.random.uniform(jax.random.fold_in(own, position), (parts,), jnp.float32, smallest / len(shards), top_value / len(shards)))
        level = level * jnp.repeat(heights, dims[position] // parts).reshape([-1 if axis == position else 1 for axis in range(len(dims))])
    return level


def shared_out(own_key, own, number, rows, number_of, top, most, skew):
    ranking = jax.random.permutation(own_key, number_of)
    heavy_load, ordinary = load_shares(number_of, rows * top, most, skew, True), load_shares(number_of, rows * top, most, skew, False)
    places = jnp.arange(number_of)

    def named(tallies, turn):
        used = int((tallies > 0).sum())
        fixed = max(1, used // 4)
        passed = fixed + (places - fixed + turn * (used - fixed)) % max(1, number_of - fixed)
        return jnp.zeros((number_of,), jnp.int32).at[ranking[jnp.where(places < fixed, places, passed)]].set(jnp.asarray(tallies, jnp.int32))

    tallies = jnp.where(number % 4 == 0, named(heavy_load, number // 4), named(ordinary, number - number // 4 - 1))
    mixed = jax.random.permutation(jax.random.fold_in(own, 3), number_of)
    source_of, receiver = mixed[0:number_of // 2 * 2:2], mixed[1:number_of // 2 * 2:2]
    margin = jnp.minimum(tallies[source_of] - 1, most - tallies[receiver]) // 2
    margin = jnp.where((source_of == ranking[0]) | (receiver == ranking[0]) | (tallies[receiver] == 0), 0, jnp.maximum(margin, 0))
    passed = jax.random.randint(jax.random.fold_in(own, 4), (number_of // 2,), 0, 1 << 20) % (margin + 1)
    tallies = tallies.at[source_of].add(-passed).at[receiver].add(passed)
    members = jnp.searchsorted(jnp.cumsum(tallies), jnp.arange(rows * top), side="right").astype(jnp.int32)
    table = members.reshape(top, rows).T
    table = table[jax.random.permutation(jax.random.fold_in(own, 1), rows)]
    turn = jax.random.randint(jax.random.fold_in(own, 2), (rows, 1), 0, top)
    return jnp.take_along_axis(table, (jnp.arange(top)[None, :] + turn) % top, axis=1)


def load_shares(count, total, limit, lean, full):
    loads = [(1 << 20) // math.isqrt(grade ** lean) + 1 for grade in range(1, count + 1)]
    largest = limit if full else min(limit, max(-(-total // count), total * loads[0] // sum(loads)))
    least = 1 if total - largest >= count - 1 else 0
    given, surplus = [largest] + [least] * (count - 1), total - largest - least * (count - 1)
    while surplus > 0:
        movable = [i for i in range(1, count) if given[i] < largest] or [i for i in range(1, count) if given[i] < limit]
        pool, budget = sum([loads[i] for i in movable]), surplus
        for i in movable:
            addition = min(limit - given[i], max(1, budget * loads[i] // pool), surplus)
            given[i] = given[i] + addition
            surplus = surplus - addition
    return np.array(given)


def noise(key, dims, scale, limit, split=(), held_as=jnp.bfloat16):
    result = jax.random.normal(key, dims, jnp.float32) * scale
    if len(split) > 0:
        result = block_levels(key, dims, split, -0.22, 0.18) * result
    return jnp.clip(result, min=-limit, max=limit).astype(held_as)


def setup_inputs(seed: int = 0) -> dict:
    splits = jax.random.split(jax.random.key(seed), 13)
    rhs_leafs = noise(splits[0], (TOTAL, NRHS), 1.0, 6.0, ((0, 512),))
    rhs_mid = noise(splits[1], (TOTAL, NRHS), 1.0, 6.0, ((0, 512),))
    rhs_root = noise(splits[2], (TOTAL, NRHS), 1.0, 6.0, ((0, 512),))
    inv_leafs = noise(splits[3], (TOTAL, N_ROW * N_COL, W_LEAF // (N_ROW * N_COL)), W_LEAF ** -0.5, 0.09375, ((0, 16), (1, 32)))
    inv_mid = noise(splits[4], (TOTAL, N_ROW * N_COL, W_MID // (N_ROW * N_COL)), W_MID ** -0.5, 0.0625, ((0, 16), (1, 32)))
    inv_root = noise(splits[5], (TOTAL, N_ROW * N_COL, W_ROOT // (N_ROW * N_COL)), W_ROOT ** -0.5, 0.046875, ((0, 16), (1, 32)))
    off_leafs = noise(splits[6], (OFF_LEAF * N_LEAF, N_ROW * N_COL, W_LEAF // (N_ROW * N_COL)), W_LEAF ** -0.5, 0.09375, ((0, 16), (1, 32)))
    off_mid = noise(splits[7], (OFF_LEAF * N_LEAF, N_ROW * N_COL, W_MID // (N_ROW * N_COL)), W_MID ** -0.5, 0.0625, ((0, 16), (1, 32)))
    owner_leafs_keys = jax.random.split(jax.random.fold_in(splits[8], 1), (OFF_LEAF * N_LEAF) // OFF_LEAF)
    owner_leafs_turns = jax.random.permutation(jax.random.fold_in(splits[8], 3), (OFF_LEAF * N_LEAF) // OFF_LEAF)
    owner_leafs = jax.vmap(lambda own, number: shared_out(jax.random.fold_in(splits[8], 2), own, number, OFF_LEAF, N_ROW * N_COL, 1, CAP, 2))(owner_leafs_keys, owner_leafs_turns).reshape((OFF_LEAF * N_LEAF, 1))
    offset_leafs = touch_ends(jax.random.randint(splits[9], (OFF_LEAF * N_LEAF,), 0, 2 * ROWS_DEV), jax.random.fold_in(splits[9], 1), 0, (2 * ROWS_DEV) - 1).astype(jnp.int32)
    owner_mid_keys = jax.random.split(jax.random.fold_in(splits[10], 1), (OFF_LEAF * N_LEAF) // OFF_LEAF)
    owner_mid_turns = jax.random.permutation(jax.random.fold_in(splits[10], 3), (OFF_LEAF * N_LEAF) // OFF_LEAF)
    owner_mid = jax.vmap(lambda own, number: shared_out(jax.random.fold_in(splits[10], 2), own, number, OFF_LEAF, N_ROW * N_COL, 1, CAP, 2))(owner_mid_keys, owner_mid_turns).reshape((OFF_LEAF * N_LEAF, 1))
    offset_mid = touch_ends(jax.random.randint(splits[11], (OFF_LEAF * N_LEAF,), 0, ROWS_DEV), jax.random.fold_in(splits[11], 1), 0, ROWS_DEV - 1).astype(jnp.int32)
    return dict(rhs_leafs=rhs_leafs, rhs_mid=rhs_mid, rhs_root=rhs_root, inv_leafs=inv_leafs, inv_mid=inv_mid, inv_root=inv_root, off_leafs=off_leafs, off_mid=off_mid, owner_leafs=owner_leafs, offset_leafs=offset_leafs, owner_mid=owner_mid, offset_mid=offset_mid)


CONTRACT_ROWS = (((0,), (0,)), ((), ()))


def to_storage(vector, groups, blocks):
    return vector.reshape(groups, blocks, ROWS_DEV, -1).transpose(1, 0, 2, 3).reshape(groups * blocks * ROWS_DEV, -1)


def to_natural(vector, groups, blocks):
    return vector.reshape(blocks, groups, ROWS_DEV, -1).transpose(1, 0, 2, 3).reshape(groups * blocks * ROWS_DEV, -1)


def forward_solve(inverse, vector, tier_level):
    node_count = 2 ** tier_level
    groups = N_LEAF // node_count
    blocks = N_ROW * N_COL
    node_rows = inverse.shape[0] // node_count
    block_span = groups * ROWS_DEV
    results = []
    for supernode in range(node_count):
        panels = inverse[supernode * node_rows:(supernode + 1) * node_rows].reshape(node_rows, blocks * block_span)
        stored = to_storage(vector[supernode * node_rows:(supernode + 1) * node_rows], groups, blocks)

        def add_block(block_index, running, panels=panels, stored=stored):
            first_col = jnp.asarray(block_index, jnp.int32) * block_span
            columns = lax.dynamic_slice_in_dim(panels, first_col, block_span, 1)
            rows_block = lax.dynamic_slice_in_dim(stored, first_col, block_span, 0)
            product = jnp.dot(columns, rows_block, preferred_element_type=jnp.float32)
            rounded = lax.optimization_barrier(product.astype(jnp.bfloat16))
            return running + rounded.astype(jnp.float32)

        running = lax.fori_loop(0, blocks, add_block, jnp.zeros((node_rows, vector.shape[1]), jnp.float32))
        results.append(running.astype(jnp.bfloat16))
    return jnp.concatenate(results, 0)


def backward_solve(inverse, vector, tier_level):
    node_count = 2 ** tier_level
    groups = N_LEAF // node_count
    blocks = N_ROW * N_COL
    node_rows = inverse.shape[0] // node_count
    results = []
    for supernode in range(node_count):
        panels = inverse[supernode * node_rows:(supernode + 1) * node_rows].reshape(node_rows, node_rows)
        transposed = lax.dot_general(panels, vector[supernode * node_rows:(supernode + 1) * node_rows], CONTRACT_ROWS, preferred_element_type=jnp.float32)
        results.append(to_natural(transposed, groups, blocks).astype(jnp.bfloat16))
    return jnp.concatenate(results, 0)


def target_rows(owner_ids, offset):
    leaf_of_row = jnp.arange(owner_ids.shape[0], dtype=jnp.int32) // OFF_LEAF
    return ((offset // ROWS_DEV) * TOTAL + leaf_of_row * (N_ROW * N_COL * ROWS_DEV) + owner_ids[:, 0] * ROWS_DEV + offset % ROWS_DEV).astype(jnp.int32)


def carry_down(off_panel, owner_ids, offset, solved, tier_level, stacked_rows):
    node_count = 2 ** tier_level
    groups = N_LEAF // node_count
    blocks = N_ROW * N_COL
    node_rows = solved.shape[0] // node_count
    off_rows = off_panel.shape[0] // node_count
    products = []
    for supernode in range(node_count):
        panels = off_panel[supernode * off_rows:(supernode + 1) * off_rows].reshape(off_rows, node_rows)
        stored = to_storage(solved[supernode * node_rows:(supernode + 1) * node_rows], groups, blocks)
        products.append(jnp.dot(panels, stored, preferred_element_type=jnp.float32))
    products = jnp.concatenate(products, 0)
    target = target_rows(owner_ids, offset)
    return jnp.zeros((stacked_rows, solved.shape[1]), jnp.float32).at[target].add(products)


def carry_up(off_panel, owner_ids, offset, stacked, tier_level):
    node_count = 2 ** tier_level
    groups = N_LEAF // node_count
    blocks = N_ROW * N_COL
    node_rows = TOTAL // node_count
    off_rows = off_panel.shape[0] // node_count
    chosen = jnp.take(stacked, target_rows(owner_ids, offset), axis=0)
    results = []
    for supernode in range(node_count):
        panels = off_panel[supernode * off_rows:(supernode + 1) * off_rows].reshape(off_rows, node_rows)
        transposed = lax.dot_general(panels, chosen[supernode * off_rows:(supernode + 1) * off_rows], CONTRACT_ROWS, preferred_element_type=jnp.float32)
        results.append(to_natural(transposed, groups, blocks))
    return jnp.concatenate(results, 0)


def reference(rhs_leafs, rhs_mid, rhs_root, inv_leafs, inv_mid, inv_root, off_leafs, off_mid, owner_leafs, offset_leafs, owner_mid, offset_mid):
    solved_leafs = forward_solve(inv_leafs, rhs_leafs, 2)
    carried_leafs = carry_down(off_leafs, owner_leafs, offset_leafs, solved_leafs, 2, 2 * TOTAL)
    input_mid = (rhs_mid.astype(jnp.float32) - carried_leafs[:TOTAL]).astype(jnp.bfloat16)
    solved_mid = forward_solve(inv_mid, input_mid, 1)
    carried_mid = carry_down(off_mid, owner_mid, offset_mid, solved_mid, 1, TOTAL)
    input_root = (rhs_root.astype(jnp.float32) - carried_leafs[TOTAL:] - carried_mid).astype(jnp.bfloat16)
    solved_root = forward_solve(inv_root, input_root, 0)
    solution_root = backward_solve(inv_root, solved_root, 0)
    back_mid = carry_up(off_mid, owner_mid, offset_mid, solution_root, 1)
    rest_mid = (solved_mid.astype(jnp.float32) - back_mid).astype(jnp.bfloat16)
    solution_mid = backward_solve(inv_mid, rest_mid, 1)
    stacked = jnp.concatenate([solution_mid, solution_root], 0)
    back_leafs = carry_up(off_leafs, owner_leafs, offset_leafs, stacked, 2)
    rest_leafs = (solved_leafs.astype(jnp.float32) - back_leafs).astype(jnp.bfloat16)
    solution_leafs = backward_solve(inv_leafs, rest_leafs, 2)
    return solution_leafs, solution_mid, solution_root
```

```python
import functools

import jax
import jax.numpy as jnp
from jax import lax
from jax.experimental import pallas as pl
from jax.experimental.pallas import tpu as pltpu
from jax.sharding import PartitionSpec as P

MESH = pl.DeviceIdType.MESH
BF = jnp.bfloat16
F32 = jnp.float32
ROWS = 32
NRHS = 256
PARTS = 1
CHUNK = 1


def z_order(nz):
    order = []
    for near in range(nz // 2, 0, -1):
        order.append(near)
        if nz - near != near:
            order.append(nz - near)
    return order + [0]


def dot(a, b):
    return jnp.dot(a, b, preferred_element_type=F32)


def dot_nt(a, b):
    return lax.dot_general(a, b, (((1,), (1,)), ((), ())), preferred_element_type=F32)


def one_hot(condition):
    return jnp.where(condition, 1.0, 0.0).astype(BF)


def kernel(sizes, *refs):
    names, groups, nz, nx = sizes
    r = dict(zip(names, refs, strict=True))
    width = NRHS // PARTS
    leaf, z, x = lax.axis_index("leaf"), lax.axis_index("row"), lax.axis_index("col")
    order = z_order(nz)
    rows = nz * nx * ROWS
    nleaf = groups[4]

    loads = {}
    for number, name in enumerate(("rl", "i1", "w1", "o1", "f1", "rm", "i2", "rr", "w2", "o2", "f2", "i3")):
        loads[name] = pltpu.make_async_copy(r["in_" + name], r["v_" + name], r["load"].at[number])
        loads[name].start()

    barrier = pltpu.get_barrier_semaphore()
    for d in range(1, nleaf):
        pl.semaphore_signal(barrier, inc=1, device_id=(lax.rem(leaf + d, nleaf), z, x), device_id_type=MESH)
    for d in range(1, nz):
        pl.semaphore_signal(barrier, inc=1, device_id=(leaf, lax.rem(z + d, nz), x), device_id_type=MESH)
    for d in range(1, nx):
        pl.semaphore_signal(barrier, inc=1, device_id=(leaf, z, lax.rem(x + d, nx)), device_id_type=MESH)

    def send(source, target, send_sem, recv_sem, where):
        pltpu.make_async_remote_copy(
            src_ref=source, dst_ref=target, send_sem=send_sem, recv_sem=recv_sem, device_id=where, device_id_type=MESH
        ).start()

    def wait(ref, sem):
        pltpu.make_async_copy(ref, ref, sem).wait()

    def member(k):
        return lax.rem(leaf, groups[k])

    def columns(h):
        return slice(h * width, (h + 1) * width)

    def gather_start(k, h, block):
        count, me, buf = groups[k], member(k), r[f"gat{k}"]
        buf[h, me] = block
        for d in range(1, count):
            there = leaf - me + lax.rem(me + d, count)
            send(buf.at[h, me], buf.at[h, me], r["gs"].at[k, h], r["gr"].at[k, h], (there, z, x))

    def multiply_start(k, h, panel):
        count, buf, prod, land = groups[k], r[f"gat{k}"], r[f"prod{k}"], r[f"rx{k}"]
        wait(buf.at[h, 0 : count - 1], r["gr"].at[k, h])
        vector = buf[h].reshape(count * ROWS, width)
        for pos, j in enumerate(order):
            there = lax.rem(z + j, nz)
            first = pl.multiple_of(there * (nx * ROWS), nx * ROWS)
            block = dot(panel[pl.ds(first, nx * ROWS), :], vector).astype(BF)
            for c in range(nx):
                prod[h, c, pos] = block[c * ROWS : (c + 1) * ROWS]
            if (pos + 1) % CHUNK == 0:
                cut = pl.ds(pos + 1 - CHUNK, CHUNK)
                for d in range(1, nx):
                    c = lax.rem(x + d, nx)
                    send(prod.at[h, c, cut], land.at[h, d - 1, cut], r["xs"].at[k, h], r["xr"].at[k, h, pos // CHUNK], (leaf, z, c))

    def reduce_x(k, h):
        prod, land, sums, final = r[f"prod{k}"], r[f"rx{k}"], r[f"sum{k}"], r[f"rz{k}"]
        own = None
        for pos, j in enumerate(order):
            if pos % CHUNK == 0:
                cut = pl.ds(pos, CHUNK)
                wait(land.at[h, :, cut], r["xr"].at[k, h, pos // CHUNK])
            total = prod[h, x, pos].astype(F32)
            for d in range(1, nx):
                total += land[h, d - 1, pos].astype(F32)
            if j == 0:
                own = total
            else:
                sums[h, pos] = total.astype(BF)
                send(sums.at[h, pos], final.at[h, j - 1], r["zs"].at[k, h], r["zr"].at[k, h], (leaf, lax.rem(z + j, nz), x))
        return own

    def reduce_z(k, h, own):
        final = r[f"rz{k}"]
        wait(final.at[h], r["zr"].at[k, h])
        total = own
        for j in range(1, nz):
            total += final[h, j - 1].astype(F32)
        return total

    def forward_sent(k):
        for h in range(PARTS):
            wait(r[f"gat{k}"].at[h, 0 : groups[k] - 1], r["gs"].at[k, h])
            wait(r[f"rx{k}"].at[h], r["xs"].at[k, h])
            wait(r[f"rz{k}"].at[h], r["zs"].at[k, h])

    def spread_x(k, h, row):
        buf = r[f"all{k}"]
        for d in range(1, nx):
            send(buf.at[h, row, x], buf.at[h, row, x], r["bxs"].at[k, h], r["bxr"].at[k, h], (leaf, z, lax.rem(x + d, nx)))

    def spread_start(k, h, block):
        buf = r[f"all{k}"]
        buf[h, z, x] = block
        for j in order[:-1]:
            send(buf.at[h, z, x], buf.at[h, z, x], r["bzs"].at[k, h], r["bzr"].at[k, h, j - 1], (leaf, lax.rem(z + j, nz), x))
        spread_x(k, h, z)

    def spread_on(k, h):
        buf = r[f"all{k}"]
        for j in reversed(order[:-1]):
            row = lax.rem(z + nz - j, nz)
            wait(buf.at[h, row, x], r["bzr"].at[k, h, j - 1])
            spread_x(k, h, row)

    def transposed_start(k, h, panel):
        buf, part, exact, land, count, me = r[f"all{k}"], r[f"part{k}"], r[f"exact{k}"], r[f"lr{k}"], groups[k], member(k)
        wait(buf.at[h, :, 0 : nx - 1], r["bxr"].at[k, h])
        result = dot(panel[...], buf[h].reshape(rows, width)).reshape(count, ROWS, width)
        exact[h] = result
        part[h] = result.astype(BF)
        for d in range(1, count):
            m = lax.rem(me + d, count)
            send(part.at[h, m], land.at[h, d - 1], r["ls"].at[k, h], r["lr"].at[k, h], (leaf - me + m, z, x))

    def transposed_end(k, h):
        exact, land = r[f"exact{k}"], r[f"lr{k}"]
        wait(land.at[h], r["lr"].at[k, h])
        total = exact[h, member(k)]
        for d in range(1, groups[k]):
            total += land[h, d - 1].astype(F32)
        return total

    def backward_sent(k):
        for h in range(PARTS):
            wait(r[f"all{k}"].at[h, 0 : nz - 1, 0], r["bzs"].at[k, h])
            wait(r[f"all{k}"].at[h, :, 0 : nx - 1], r["bxs"].at[k, h])
            wait(r[f"lr{k}"].at[h], r["ls"].at[k, h])

    def slots(name):
        ids = r["v_w" + name][...]
        places = ids.shape[1]
        blocks = nz * nx
        mine = jnp.broadcast_to(ids, (blocks, places)) == lax.broadcasted_iota(jnp.int32, (blocks, places), 0)
        before = lax.broadcasted_iota(jnp.int32, (places, places), 0) < lax.broadcasted_iota(jnp.int32, (places, places), 1)
        rank = jnp.where(mine, dot(one_hot(mine), one_hot(before)), -1.0)
        slot = lax.broadcasted_iota(jnp.int32, (ROWS, places), 0).astype(F32)
        for b in range(blocks):
            r["perm"][b] = one_hot(jnp.broadcast_to(rank[b : b + 1, :], (ROWS, places)) == slot)
        r["p" + name][...] = dot(r["perm"][...].reshape(blocks * ROWS, places), r["v_o" + name][...]).astype(BF)
        own = r["perm"][z * nx + x]
        targets = r["lay" + name].shape[0]
        offset = jnp.broadcast_to(r["v_f" + name][...], (targets, places))
        wanted = one_hot(offset == lax.broadcasted_iota(jnp.int32, (targets, places), 0))
        r["lay" + name][...] = dot_nt(wanted, own).astype(BF)
        r["sel" + name][...] = dot_nt(own, wanted).astype(BF)

    def to_targets(name, total):
        high = total.astype(BF)
        low = (total - high.astype(F32)).astype(BF)
        return dot(r["lay" + name][...], high) + dot(r["lay" + name][...], low)

    def transpose(name, panel):
        r["t_" + name][...] = panel[...].T

    halves = range(PARTS)

    def forward(k, blocks, panel, after_gather=None, after_x=None):
        for h in halves:
            gather_start(k, h, blocks[h])
        if after_gather is not None:
            after_gather()
        for h in halves:
            multiply_start(k, h, panel)
        if after_x is not None:
            after_x()
        own = [reduce_x(k, h) for h in halves]
        return [reduce_z(k, h, own[h]) for h in halves]

    def backward(k, blocks, panel, before=None):
        for h in halves:
            spread_start(k, h, blocks[h])
        for h in halves:
            spread_on(k, h)
        if before is not None:
            before()
        for h in halves:
            transposed_start(k, h, panel)
        return [transposed_end(k, h) for h in halves]

    def load(*wanted):
        for name in wanted:
            loads[name].wait()

    load("rl")
    pl.semaphore_wait(barrier, nleaf + nz + nx - 3)

    def prepare_leafs():
        load("w1", "o1", "f1")
        slots("1")

    def prepare_mid():
        load("w2", "o2", "f2")
        slots("2")

    total = forward(0, [r["v_rl"][:, columns(h)] for h in halves], r["v_i1"], lambda: load("i1"), prepare_leafs)
    solved_leafs = [t.astype(BF) for t in total]
    total = forward(1, solved_leafs, r["p1"], None, prepare_mid)
    carried = [to_targets("1", t) for t in total]
    load("rm")
    blocks = [(r["v_rm"][:, columns(h)].astype(F32) - carried[h][:ROWS]).astype(BF) for h in halves]
    total = forward(2, blocks, r["v_i2"], lambda: load("i2"), lambda: transpose("p1", r["p1"]))
    solved_mid = [t.astype(BF) for t in total]
    total = forward(3, solved_mid, r["p2"], None, lambda: transpose("p2", r["p2"]))
    load("rr")
    blocks = [
        (r["v_rr"][:, columns(h)].astype(F32) - carried[h][ROWS:] - to_targets("2", total[h])).astype(BF) for h in halves
    ]
    load("i3")
    total = forward(4, blocks, r["v_i3"], lambda: transpose("i3", r["v_i3"]), lambda: transpose("i2", r["v_i2"]))

    total = backward(4, [t.astype(BF) for t in total], r["t_i3"], lambda: transpose("i1", r["v_i1"]))
    solution_root = [t.astype(BF) for t in total]
    for h in halves:
        r["out_r"][:, columns(h)] = solution_root[h]
    total = backward(3, [dot(r["sel2"][...], solution_root[h]).astype(BF) for h in halves], r["t_p2"])
    rest = [(solved_mid[h].astype(F32) - total[h]).astype(BF) for h in halves]
    total = backward(2, rest, r["t_i2"])
    solution_mid = [t.astype(BF) for t in total]
    for h in halves:
        r["out_m"][:, columns(h)] = solution_mid[h]
    stacked = [jnp.concatenate([solution_mid[h], solution_root[h]], 0) for h in halves]
    total = backward(1, [dot(r["sel1"][...], stacked[h]).astype(BF) for h in halves], r["t_p1"])
    rest = [(solved_leafs[h].astype(F32) - total[h]).astype(BF) for h in halves]
    total = backward(0, rest, r["t_i1"])
    for h in halves:
        r["out_l"][:, columns(h)] = total[h].astype(BF)

    for k in range(5):
        forward_sent(k)
        backward_sent(k)


def shards(
    mesh_shape,
    rhs_leafs,
    rhs_mid,
    rhs_root,
    inv_leafs,
    inv_mid,
    inv_root,
    off_leafs,
    off_mid,
    owner_leafs,
    offset_leafs,
    owner_mid,
    offset_mid,
):
    nleaf, nz, nx = mesh_shape
    groups = (nleaf // 4, nleaf // 4, nleaf // 2, nleaf // 2, nleaf)
    width = NRHS // PARTS
    rows = nz * nx * ROWS

    def flat(panel):
        return panel.reshape(panel.shape[0], panel.shape[2])

    operands = {
        "rl": rhs_leafs,
        "rm": rhs_mid,
        "rr": rhs_root,
        "i1": flat(inv_leafs),
        "i2": flat(inv_mid),
        "i3": flat(inv_root),
        "o1": flat(off_leafs),
        "o2": flat(off_mid),
        "w1": owner_leafs.reshape(1, -1),
        "f1": offset_leafs.reshape(1, -1),
        "w2": owner_mid.reshape(1, -1),
        "f2": offset_mid.reshape(1, -1),
    }
    places = off_leafs.shape[0]
    names = ["in_" + name for name in operands] + ["out_l", "out_m", "out_r"]
    scratch = []

    def keep(name, shape, dtype=BF):
        names.append(name)
        scratch.append(pltpu.VMEM(shape, dtype))

    def semaphores(name, shape):
        names.append(name)
        scratch.append(pltpu.SemaphoreType.DMA(shape))

    for name, value in operands.items():
        keep("v_" + name, value.shape, value.dtype)
    semaphores("load", (len(operands),))
    keep("perm", (nz * nx, ROWS, places))
    for name, panel, targets in (("1", operands["o1"], 2 * ROWS), ("2", operands["o2"], ROWS)):
        keep("p" + name, (rows, panel.shape[1]))
        keep("t_p" + name, (panel.shape[1], rows))
        keep("lay" + name, (targets, ROWS))
        keep("sel" + name, (ROWS, targets))
    for name in ("i1", "i2", "i3"):
        keep("t_" + name, operands[name].shape[::-1])
    for k, count in enumerate(groups):
        keep(f"gat{k}", (PARTS, count, ROWS, width))
        keep(f"prod{k}", (PARTS, nx, nz, ROWS, width))
        keep(f"rx{k}", (PARTS, nx - 1, nz, ROWS, width))
        keep(f"sum{k}", (PARTS, nz, ROWS, width))
        keep(f"rz{k}", (PARTS, nz - 1, ROWS, width))
        keep(f"all{k}", (PARTS, nz, nx, ROWS, width))
        keep(f"part{k}", (PARTS, count, ROWS, width))
        keep(f"exact{k}", (PARTS, count, ROWS, width), F32)
        keep(f"lr{k}", (PARTS, count - 1, ROWS, width))
    for name in ("gs", "gr", "xs", "zs", "zr", "bzs", "bxs", "bxr", "ls", "lr"):
        semaphores(name, (5, PARTS))
    semaphores("xr", (5, PARTS, nz // CHUNK))
    semaphores("bzr", (5, PARTS, nz - 1))

    block = jax.ShapeDtypeStruct(rhs_leafs.shape, rhs_leafs.dtype)
    return pl.pallas_call(
        functools.partial(kernel, (tuple(names), groups, nz, nx)),
        out_shape=(block, block, block),
        in_specs=[pl.BlockSpec(memory_space=pl.ANY)] * len(operands),
        out_specs=[pl.BlockSpec(memory_space=pltpu.VMEM)] * 3,
        scratch_shapes=scratch,
        compiler_params=pltpu.CompilerParams(collective_id=0, has_side_effects=True, vmem_limit_bytes=50 * 2**20),
        cost_estimate=pl.CostEstimate(flops=1_200_000_000, bytes_accessed=2_400_000, transcendentals=0),
        name="triangular_solve",
    )(*operands.values())


def solution(mesh):
    vector = P(("leaf", "row", "col"), None)
    panel = P("leaf", ("row", "col"), None)
    return jax.shard_map(
        functools.partial(shards, (mesh.shape["leaf"], mesh.shape["row"], mesh.shape["col"])),
        mesh=mesh,
        in_specs=(vector,) * 3 + (panel,) * 5 + (P("leaf", None), P("leaf")) * 2,
        out_specs=(vector,) * 3,
        check_vma=False,
    )
```

```python
import functools

import jax
import jax.numpy as jnp
from jax import lax
from jax.experimental import pallas as pl
from jax.experimental.pallas import tpu as pltpu
from jax.sharding import PartitionSpec as P

MESH = pl.DeviceIdType.MESH
BF = jnp.bfloat16
F32 = jnp.float32
ROWS = 32
NRHS = 256
PARTS = 2
CHUNK = 1
LEAD = 1


def z_order(nz):
    order = []
    for near in range(nz // 2, 0, -1):
        order.append(near)
        if nz - near != near:
            order.append(nz - near)
    return order + [0]


def dot(a, b):
    return jnp.dot(a, b, preferred_element_type=F32)


def dot_nt(a, b):
    return lax.dot_general(a, b, (((1,), (1,)), ((), ())), preferred_element_type=F32)


def one_hot(condition):
    return jnp.where(condition, 1.0, 0.0).astype(BF)


def kernel(sizes, *refs):
    names, groups, nz, nx = sizes
    r = dict(zip(names, refs, strict=True))
    width = NRHS // PARTS
    leaf, z, x = lax.axis_index("leaf"), lax.axis_index("row"), lax.axis_index("col")
    order = z_order(nz)
    rows = nz * nx * ROWS
    nleaf = groups[4]
    y_order = z_order(nleaf // 2)
    x_order = z_order(nx)[:-1]
    sibling = leaf + 1 - 2 * lax.rem(leaf, 2)

    loads = {}
    for number, name in enumerate(("rl", "i1", "w1", "o1", "f1", "rm", "i2", "rr", "w2", "o2", "f2", "i3")):
        loads[name] = pltpu.make_async_copy(r["in_" + name], r["v_" + name], r["load"].at[number])
        loads[name].start()

    barrier = pltpu.get_barrier_semaphore()
    for d in range(1, nleaf):
        pl.semaphore_signal(barrier, inc=1, device_id=(lax.rem(leaf + d, nleaf), z, x), device_id_type=MESH)
    for d in range(1, nz):
        pl.semaphore_signal(barrier, inc=1, device_id=(leaf, lax.rem(z + d, nz), x), device_id_type=MESH)
    for d in range(1, nx):
        pl.semaphore_signal(barrier, inc=1, device_id=(leaf, z, lax.rem(x + d, nx)), device_id_type=MESH)

    def send(source, target, send_sem, recv_sem, where):
        pltpu.make_async_remote_copy(
            src_ref=source, dst_ref=target, send_sem=send_sem, recv_sem=recv_sem, device_id=where, device_id_type=MESH
        ).start()

    def wait(ref, sem):
        pltpu.make_async_copy(ref, ref, sem).wait()

    def member(k):
        return lax.rem(leaf, groups[k])

    def columns(h):
        return slice(h * width, (h + 1) * width)

    def is_wide(k):
        return groups[k] == nleaf

    def gather_start(k, h, block):
        count, me, buf = groups[k], member(k), r[f"gat{k}"]
        buf[h, me] = block
        if is_wide(k):
            own = buf.at[h, me]
            for d in y_order[:-1]:
                send(own, own, r["gs"].at[k, h], r["gyr"].at[h, d - 1], (lax.rem(leaf + 2 * d, nleaf), z, x))
            send(own, own, r["gs"].at[k, h], r["gr"].at[k, h], (sibling, z, x))
            return
        for d in range(1, count):
            there = leaf - me + lax.rem(me + d, count)
            send(buf.at[h, me], buf.at[h, me], r["gs"].at[k, h], r["gr"].at[k, h], (there, z, x))

    def gather_wait(k, h):
        count, buf = groups[k], r[f"gat{k}"]
        if is_wide(k):
            for d in reversed(y_order[:-1]):
                m = lax.rem(leaf + nleaf - 2 * d, nleaf)
                wait(buf.at[h, m], r["gyr"].at[h, d - 1])
                send(buf.at[h, m], buf.at[h, m], r["gs"].at[k, h], r["gr"].at[k, h], (sibling, z, x))
            wait(buf.at[h, 0 : nleaf // 2], r["gr"].at[k, h])
        else:
            wait(buf.at[h, 0 : count - 1], r["gr"].at[k, h])

    def multiply_start(k, h, panel):
        count, buf, prod, land = groups[k], r[f"gat{k}"], r[f"prod{k}"], r[f"rx{k}"]
        vector = buf[h].reshape(count * ROWS, width)
        for pos, j in enumerate(order):
            there = lax.rem(z + j, nz)
            first = pl.multiple_of(there * (nx * ROWS), nx * ROWS)
            block = dot(panel[pl.ds(first, nx * ROWS), :], vector).astype(BF)
            for c in range(nx):
                prod[h, c, pos] = block[c * ROWS : (c + 1) * ROWS]
            if (pos + 1) % CHUNK == 0:
                cut = pl.ds(pos + 1 - CHUNK, CHUNK)
                for d in x_order:
                    c = lax.rem(x + d, nx)
                    send(prod.at[h, c, cut], land.at[h, d - 1, cut], r["xs"].at[k, h], r["xr"].at[k, h, pos // CHUNK], (leaf, z, c))

    def reduce_x(k, h):
        prod, land, sums, final = r[f"prod{k}"], r[f"rx{k}"], r[f"sum{k}"], r[f"rz{k}"]
        own = None
        for pos, j in enumerate(order):
            if pos % CHUNK == 0:
                cut = pl.ds(pos, CHUNK)
                wait(land.at[h, :, cut], r["xr"].at[k, h, pos // CHUNK])
            total = prod[h, x, pos].astype(F32)
            for d in range(1, nx):
                total += land[h, d - 1, pos].astype(F32)
            if j == 0:
                own = total
            else:
                sums[h, pos] = total.astype(BF)
                send(sums.at[h, pos], final.at[h, j - 1], r["zs"].at[k, h], r["zr"].at[k, h], (leaf, lax.rem(z + j, nz), x))
        return own

    def reduce_z(k, h, own):
        final = r[f"rz{k}"]
        wait(final.at[h], r["zr"].at[k, h])
        total = own
        for j in range(1, nz):
            total += final[h, j - 1].astype(F32)
        return total

    def forward(k, h, block, panel, ready=None):
        gather_start(k, h, block)
        yield
        gather_wait(k, h)
        if ready is not None:
            ready()
        multiply_start(k, h, panel)
        yield
        own = reduce_x(k, h)
        yield
        return reduce_z(k, h, own)

    def forward_sent(k, h):
        wait(r[f"gat{k}"].at[h, 0 : groups[k] - 1], r["gs"].at[k, h])
        wait(r[f"rx{k}"].at[h], r["xs"].at[k, h])
        wait(r[f"rz{k}"].at[h], r["zs"].at[k, h])

    def spread_x(k, h, row):
        buf = r[f"all{k}"]
        for d in x_order:
            send(buf.at[h, row, x], buf.at[h, row, x], r["bxs"].at[k, h], r["bxr"].at[k, h], (leaf, z, lax.rem(x + d, nx)))

    def spread_start(k, h, block):
        buf = r[f"all{k}"]
        buf[h, z, x] = block
        for j in order[:-1]:
            send(buf.at[h, z, x], buf.at[h, z, x], r["bzs"].at[k, h], r["bzr"].at[k, h, j - 1], (leaf, lax.rem(z + j, nz), x))
        spread_x(k, h, z)

    def spread_on(k, h):
        buf = r[f"all{k}"]
        for j in reversed(order[:-1]):
            row = lax.rem(z + nz - j, nz)
            wait(buf.at[h, row, x], r["bzr"].at[k, h, j - 1])
            spread_x(k, h, row)

    def transposed_start(k, h, panel):
        buf, part, exact, land, count, me = r[f"all{k}"], r[f"part{k}"], r[f"exact{k}"], r[f"lr{k}"], groups[k], member(k)
        wait(buf.at[h, :, 0 : nx - 1], r["bxr"].at[k, h])
        result = dot(panel[...], buf[h].reshape(rows, width)).reshape(count, ROWS, width)
        exact[h] = result
        part[h] = result.astype(BF)
        if is_wide(k):
            for d in y_order:
                m = lax.rem(sibling + 2 * d, nleaf)
                send(part.at[h, m], r["pair"].at[h, d], r["ps"].at[h], r["pr"].at[h, d], (sibling, z, x))
            return
        for d in range(1, count):
            m = lax.rem(me + d, count)
            send(part.at[h, m], land.at[h, d - 1], r["ls"].at[k, h], r["lr"].at[k, h], (leaf - me + m, z, x))

    def transposed_pairs(k, h):
        exact, pair, land, sums = r[f"exact{k}"], r["pair"], r[f"lr{k}"], r["pairsum"]
        total = None
        for d in y_order:
            m = lax.rem(leaf + 2 * d, nleaf)
            wait(pair.at[h, d], r["pr"].at[h, d])
            total = exact[h, m] + pair[h, d].astype(F32)
            if d:
                sums[h, d] = total.astype(BF)
                send(sums.at[h, d], land.at[h, d - 1], r["ls"].at[k, h], r["lr"].at[k, h], (m, z, x))
        return total

    def transposed_end(k, h, own):
        land = r[f"lr{k}"]
        wait(land.at[h], r["lr"].at[k, h])
        total = own
        for d in range(land.shape[1]):
            total += land[h, d].astype(F32)
        return total

    def backward(k, h, block, panel):
        spread_start(k, h, block)
        yield
        spread_on(k, h)
        yield
        transposed_start(k, h, panel)
        yield
        if is_wide(k):
            own = transposed_pairs(k, h)
            yield
        else:
            own = r[f"exact{k}"][h, member(k)]
        return transposed_end(k, h, own)

    def backward_sent(k, h):
        wait(r[f"all{k}"].at[h, 0 : nz - 1, 0], r["bzs"].at[k, h])
        wait(r[f"all{k}"].at[h, :, 0 : nx - 1], r["bxs"].at[k, h])
        wait(r[f"lr{k}"].at[h], r["ls"].at[k, h])
        if is_wide(k):
            wait(r["pair"].at[h], r["ps"].at[h])

    def slots(name):
        ids = r["v_w" + name][...]
        places = ids.shape[1]
        blocks = nz * nx
        mine = jnp.broadcast_to(ids, (blocks, places)) == lax.broadcasted_iota(jnp.int32, (blocks, places), 0)
        before = lax.broadcasted_iota(jnp.int32, (places, places), 0) < lax.broadcasted_iota(jnp.int32, (places, places), 1)
        rank = jnp.where(mine, dot(one_hot(mine), one_hot(before)), -1.0)
        slot = lax.broadcasted_iota(jnp.int32, (ROWS, places), 0).astype(F32)
        for b in range(blocks):
            r["perm"][b] = one_hot(jnp.broadcast_to(rank[b : b + 1, :], (ROWS, places)) == slot)
        r["p" + name][...] = dot(r["perm"][...].reshape(blocks * ROWS, places), r["v_o" + name][...]).astype(BF)
        own = r["perm"][z * nx + x]
        targets = r["lay" + name].shape[0]
        offset = jnp.broadcast_to(r["v_f" + name][...], (targets, places))
        wanted = one_hot(offset == lax.broadcasted_iota(jnp.int32, (targets, places), 0))
        r["lay" + name][...] = dot_nt(wanted, own).astype(BF)
        r["sel" + name][...] = dot_nt(own, wanted).astype(BF)

    def to_targets(name, total):
        high = total.astype(BF)
        low = (total - high.astype(F32)).astype(BF)
        return dot(r["lay" + name][...], high) + dot(r["lay" + name][...], low)

    def transpose(name, panel):
        r["t_" + name][...] = panel[...].T

    loaded = set()

    def load(*wanted):
        for name in wanted:
            if name not in loaded:
                loads[name].wait()
                loaded.add(name)

    def solve(h):
        across = columns(h)
        first = h == 0
        total = yield from forward(0, h, r["v_rl"][:, across], r["v_i1"], lambda: load("i1"))
        solved_leafs = total.astype(BF)
        total = yield from forward(1, h, solved_leafs, r["p1"])
        carried = to_targets("1", total)
        load("rm")
        block = (r["v_rm"][:, across].astype(F32) - carried[:ROWS]).astype(BF)
        total = yield from forward(2, h, block, r["v_i2"], lambda: load("i2"))
        solved_mid = total.astype(BF)
        total = yield from forward(3, h, solved_mid, r["p2"])
        load("rr")
        block = (r["v_rr"][:, across].astype(F32) - carried[ROWS:] - to_targets("2", total)).astype(BF)
        total = yield from forward(4, h, block, r["v_i3"], lambda: load("i3"))

        total = yield from backward(4, h, total.astype(BF), r["t_i3"])
        solution_root = total.astype(BF)
        r["out_r"][:, across] = solution_root
        total = yield from backward(3, h, dot(r["sel2"][...], solution_root).astype(BF), r["t_p2"])
        total = yield from backward(2, h, (solved_mid.astype(F32) - total).astype(BF), r["t_i2"])
        solution_mid = total.astype(BF)
        r["out_m"][:, across] = solution_mid
        stacked = jnp.concatenate([solution_mid, solution_root], 0)
        total = yield from backward(1, h, dot(r["sel1"][...], stacked).astype(BF), r["t_p1"])
        total = yield from backward(0, h, (solved_leafs.astype(F32) - total).astype(BF), r["t_i1"])
        r["out_l"][:, across] = total.astype(BF)

    def prepare(number):
        if number == 1:
            load("w2", "o2", "f2")
            slots("2")
        elif number == 2:
            load("i1")
            transpose("i1", r["v_i1"])
            transpose("p1", r["p1"])
            transpose("p2", r["p2"])
        elif number == 4:
            load("i2", "i3")
            transpose("i2", r["v_i2"])
            transpose("i3", r["v_i3"])

    load("w1", "o1", "f1")
    slots("1")
    load("rl")
    pl.semaphore_wait(barrier, nleaf + nz + nx - 3)

    chains = [solve(h) for h in range(PARTS)]
    for h, chain in enumerate(chains):
        for _ in range(LEAD * (PARTS - 1 - h)):
            next(chain)
    running = list(chains)
    number = 0
    while running:
        for chain in list(running):
            if next(chain, running) is running:
                running.remove(chain)
        prepare(number)
        number += 1

    for k in range(5):
        for h in range(PARTS):
            forward_sent(k, h)
            backward_sent(k, h)


def shards(
    mesh_shape,
    rhs_leafs,
    rhs_mid,
    rhs_root,
    inv_leafs,
    inv_mid,
    inv_root,
    off_leafs,
    off_mid,
    owner_leafs,
    offset_leafs,
    owner_mid,
    offset_mid,
):
    nleaf, nz, nx = mesh_shape
    groups = (nleaf // 4, nleaf // 4, nleaf // 2, nleaf // 2, nleaf)
    width = NRHS // PARTS
    rows = nz * nx * ROWS

    def flat(panel):
        return panel.reshape(panel.shape[0], panel.shape[2])

    operands = {
        "rl": rhs_leafs,
        "rm": rhs_mid,
        "rr": rhs_root,
        "i1": flat(inv_leafs),
        "i2": flat(inv_mid),
        "i3": flat(inv_root),
        "o1": flat(off_leafs),
        "o2": flat(off_mid),
        "w1": owner_leafs.reshape(1, -1),
        "f1": offset_leafs.reshape(1, -1),
        "w2": owner_mid.reshape(1, -1),
        "f2": offset_mid.reshape(1, -1),
    }
    places = off_leafs.shape[0]
    names = ["in_" + name for name in operands] + ["out_l", "out_m", "out_r"]
    scratch = []

    def keep(name, shape, dtype=BF):
        names.append(name)
        scratch.append(pltpu.VMEM(shape, dtype))

    def semaphores(name, shape):
        names.append(name)
        scratch.append(pltpu.SemaphoreType.DMA(shape))

    for name, value in operands.items():
        keep("v_" + name, value.shape, value.dtype)
    semaphores("load", (len(operands),))
    keep("perm", (nz * nx, ROWS, places))
    for name, panel, targets in (("1", operands["o1"], 2 * ROWS), ("2", operands["o2"], ROWS)):
        keep("p" + name, (rows, panel.shape[1]))
        keep("t_p" + name, (panel.shape[1], rows))
        keep("lay" + name, (targets, ROWS))
        keep("sel" + name, (ROWS, targets))
    for name in ("i1", "i2", "i3"):
        keep("t_" + name, operands[name].shape[::-1])
    for k, count in enumerate(groups):
        keep(f"gat{k}", (PARTS, count, ROWS, width))
        keep(f"prod{k}", (PARTS, nx, nz, ROWS, width))
        keep(f"rx{k}", (PARTS, nx - 1, nz, ROWS, width))
        keep(f"sum{k}", (PARTS, nz, ROWS, width))
        keep(f"rz{k}", (PARTS, nz - 1, ROWS, width))
        keep(f"all{k}", (PARTS, nz, nx, ROWS, width))
        keep(f"part{k}", (PARTS, count, ROWS, width))
        keep(f"exact{k}", (PARTS, count, ROWS, width), F32)
        keep(f"lr{k}", (PARTS, (count // 2 if count == nleaf else count) - 1, ROWS, width))
    keep("pair", (PARTS, nleaf // 2, ROWS, width))
    keep("pairsum", (PARTS, nleaf // 2, ROWS, width))
    semaphores("gyr", (PARTS, nleaf // 2 - 1))
    semaphores("ps", (PARTS,))
    semaphores("pr", (PARTS, nleaf // 2))
    for name in ("gs", "gr", "xs", "zs", "zr", "bzs", "bxs", "bxr", "ls", "lr"):
        semaphores(name, (5, PARTS))
    semaphores("xr", (5, PARTS, nz // CHUNK))
    semaphores("bzr", (5, PARTS, nz - 1))

    block = jax.ShapeDtypeStruct(rhs_leafs.shape, rhs_leafs.dtype)
    return pl.pallas_call(
        functools.partial(kernel, (tuple(names), groups, nz, nx)),
        out_shape=(block, block, block),
        in_specs=[pl.BlockSpec(memory_space=pl.ANY)] * len(operands),
        out_specs=[pl.BlockSpec(memory_space=pltpu.VMEM)] * 3,
        scratch_shapes=scratch,
        compiler_params=pltpu.CompilerParams(collective_id=0, has_side_effects=True, vmem_limit_bytes=63 * 2**20),
        cost_estimate=pl.CostEstimate(flops=1_200_000_000, bytes_accessed=2_400_000, transcendentals=0),
        name="triangular_solve",
    )(*operands.values())


def solution(mesh):
    vector = P(("leaf", "row", "col"), None)
    panel = P("leaf", ("row", "col"), None)
    return jax.shard_map(
        functools.partial(shards, (mesh.shape["leaf"], mesh.shape["row"], mesh.shape["col"])),
        mesh=mesh,
        in_specs=(vector,) * 3 + (panel,) * 5 + (P("leaf", None), P("leaf")) * 2,
        out_specs=(vector,) * 3,
        check_vma=False,
    )
```

```python
import functools

import jax
import jax.numpy as jnp
from jax import lax
from jax.experimental import pallas as pl
from jax.experimental.pallas import tpu as pltpu
from jax.sharding import PartitionSpec as P

MESH = pl.DeviceIdType.MESH
BF = jnp.bfloat16
F32 = jnp.float32
ROWS = 32
NRHS = 256
PARTS = 2
CHUNK = 2
Y_FAR = 3
LEAD = 1


def z_order(nz):
    order = []
    for near in range(nz // 2, 0, -1):
        order.append(near)
        if nz - near != near:
            order.append(nz - near)
    return order + [0]


def dot(a, b):
    return jnp.dot(a, b, preferred_element_type=F32)


def dot_nt(a, b):
    return lax.dot_general(a, b, (((1,), (1,)), ((), ())), preferred_element_type=F32)


def one_hot(condition):
    return jnp.where(condition, 1.0, 0.0).astype(BF)


def kernel(sizes, *refs):
    names, groups, nz, nx = sizes
    r = dict(zip(names, refs, strict=True))
    width = NRHS // PARTS
    leaf, z, x = lax.axis_index("leaf"), lax.axis_index("row"), lax.axis_index("col")
    order = z_order(nz)
    rows = nz * nx * ROWS
    nleaf = groups[4]
    y_order = z_order(nleaf // 2)
    y_far = y_order[:Y_FAR]
    x_order = z_order(nx)[:-1]
    sibling = leaf + 1 - 2 * lax.rem(leaf, 2)

    barrier = pltpu.get_barrier_semaphore()
    for d in z_order(nz)[:-1]:
        pl.semaphore_signal(barrier, inc=1, device_id=(leaf, lax.rem(z + d, nz), x), device_id_type=MESH)
    for d in y_order[:-1]:
        for core in range(2):
            there = lax.rem(leaf - lax.rem(leaf, 2) + 2 * d + core, nleaf)
            pl.semaphore_signal(barrier, inc=1, device_id=(there, z, x), device_id_type=MESH)
    for d in range(1, nx):
        pl.semaphore_signal(barrier, inc=1, device_id=(leaf, z, lax.rem(x + d, nx)), device_id_type=MESH)
    pl.semaphore_signal(barrier, inc=1, device_id=(sibling, z, x), device_id_type=MESH)

    loads = {}
    for number, name in enumerate(("rl", "i1", "w1", "o1", "f1", "rm", "i2", "rr", "w2", "o2", "f2", "i3")):
        loads[name] = pltpu.make_async_copy(r["in_" + name], r["v_" + name], r["load"].at[number])
        loads[name].start()

    def send(source, target, send_sem, recv_sem, where):
        pltpu.make_async_remote_copy(
            src_ref=source, dst_ref=target, send_sem=send_sem, recv_sem=recv_sem, device_id=where, device_id_type=MESH
        ).start()

    def wait(ref, sem):
        pltpu.make_async_copy(ref, ref, sem).wait()

    def member(k):
        return lax.rem(leaf, groups[k])

    def columns(h):
        return slice(h * width, (h + 1) * width)

    def flipped(me, bits):
        there, bit = me, 1
        while bit <= bits:
            if bits & bit:
                there = there + bit * (1 - 2 * lax.rem(me // bit, 2))
            bit *= 2
        return there

    def flips(count):
        return sorted(range(1, count), reverse=True)

    def is_wide(k):
        return groups[k] == nleaf

    def gather_start(k, h, block):
        count, me, buf = groups[k], member(k), r[f"gat{k}"]
        buf[h, me] = block
        if is_wide(k):
            own = buf.at[h, me]
            for d in y_order[:-1]:
                send(own, own, r["gs"].at[k, h], r["gyr"].at[h, d - 1], (lax.rem(leaf + 2 * d, nleaf), z, x))
                if d in y_far:
                    send(own, own, r["gs"].at[k, h], r["gr"].at[k, h], (lax.rem(sibling + 2 * d, nleaf), z, x))
            send(own, own, r["gs"].at[k, h], r["gr"].at[k, h], (sibling, z, x))
            return
        for d in flips(count):
            send(buf.at[h, me], buf.at[h, me], r["gs"].at[k, h], r["gr"].at[k, h], (leaf - me + flipped(me, d), z, x))

    def gather_wait(k, h):
        count, buf = groups[k], r[f"gat{k}"]
        if is_wide(k):
            for d in reversed(y_order[:-1]):
                m = lax.rem(leaf + nleaf - 2 * d, nleaf)
                wait(buf.at[h, m], r["gyr"].at[h, d - 1])
                if d not in y_far:
                    send(buf.at[h, m], buf.at[h, m], r["gs"].at[k, h], r["gr"].at[k, h], (sibling, z, x))
            wait(buf.at[h, 0 : nleaf // 2], r["gr"].at[k, h])
        else:
            wait(buf.at[h, 0 : count - 1], r["gr"].at[k, h])

    def multiply_start(k, h, panel):
        count, buf, prod, land = groups[k], r[f"gat{k}"], r[f"prod{k}"], r[f"rx{k}"]
        vector = buf[h].reshape(count * ROWS, width)
        for pos, j in enumerate(order):
            there = lax.rem(z + j, nz)
            first = pl.multiple_of(there * (nx * ROWS), nx * ROWS)
            block = dot(panel[pl.ds(first, nx * ROWS), :], vector).astype(BF)
            for c in range(nx):
                prod[h, c, pos] = block[c * ROWS : (c + 1) * ROWS]
            if (pos + 1) % CHUNK == 0:
                cut = pl.ds(pos + 1 - CHUNK, CHUNK)
                for d in x_order:
                    c = lax.rem(x + d, nx)
                    send(prod.at[h, c, cut], land.at[h, d - 1, cut], r["xs"].at[k, h], r["xr"].at[k, h, pos // CHUNK], (leaf, z, c))

    def reduce_x(k, h):
        prod, land, sums, final = r[f"prod{k}"], r[f"rx{k}"], r[f"sum{k}"], r[f"rz{k}"]
        own = None
        for pos, j in enumerate(order):
            if pos % CHUNK == 0:
                cut = pl.ds(pos, CHUNK)
                wait(land.at[h, :, cut], r["xr"].at[k, h, pos // CHUNK])
            total = prod[h, x, pos].astype(F32)
            for d in range(1, nx):
                total += land[h, d - 1, pos].astype(F32)
            if j == 0:
                own = total
            else:
                sums[h, pos] = total.astype(BF)
                send(sums.at[h, pos], final.at[h, j - 1], r["zs"].at[k, h], r["zr"].at[k, h], (leaf, lax.rem(z + j, nz), x))
        return own

    def reduce_z(k, h, own):
        final = r[f"rz{k}"]
        wait(final.at[h], r["zr"].at[k, h])
        total = own
        for j in range(1, nz):
            total += final[h, j - 1].astype(F32)
        return total

    def forward(k, h, block, panel, ready=None):
        gather_start(k, h, block)
        if k:
            forward_sent(k - 1, h)
        yield
        gather_wait(k, h)
        if ready is not None:
            ready()
        multiply_start(k, h, panel)
        yield
        own = reduce_x(k, h)
        yield
        return reduce_z(k, h, own)

    def forward_sent(k, h):
        wait(r[f"gat{k}"].at[h, 0 : groups[k] - 1], r["gs"].at[k, h])
        wait(r[f"rx{k}"].at[h], r["xs"].at[k, h])
        wait(r[f"rz{k}"].at[h], r["zs"].at[k, h])

    def spread_x(k, h, row):
        buf = r[f"all{k}"]
        for d in x_order:
            send(buf.at[h, row, x], buf.at[h, row, x], r["bxs"].at[k, h], r["bxr"].at[k, h], (leaf, z, lax.rem(x + d, nx)))

    def spread_start(k, h, block):
        buf = r[f"all{k}"]
        buf[h, z, x] = block
        for j in order[:-1]:
            send(buf.at[h, z, x], buf.at[h, z, x], r["bzs"].at[k, h], r["bzr"].at[k, h, j - 1], (leaf, lax.rem(z + j, nz), x))
        spread_x(k, h, z)

    def spread_on(k, h):
        buf = r[f"all{k}"]
        for j in reversed(order[:-1]):
            row = lax.rem(z + nz - j, nz)
            wait(buf.at[h, row, x], r["bzr"].at[k, h, j - 1])
            spread_x(k, h, row)

    def transposed_start(k, h, panel):
        buf, part, exact, land, count, me = r[f"all{k}"], r[f"part{k}"], r[f"exact{k}"], r[f"lr{k}"], groups[k], member(k)
        wait(buf.at[h, :, 0 : nx - 1], r["bxr"].at[k, h])
        result = dot(panel[...], buf[h].reshape(rows, width)).reshape(count, ROWS, width)
        exact[h] = result
        part[h] = result.astype(BF)
        if is_wide(k):
            for d in y_order:
                m = lax.rem(sibling + 2 * d, nleaf)
                send(part.at[h, m], r["pair"].at[h, d], r["ps"].at[h], r["pr"].at[h, d], (sibling, z, x))
            return
        for d in flips(count):
            m = flipped(me, d)
            send(part.at[h, m], land.at[h, d - 1], r["ls"].at[k, h], r["lr"].at[k, h], (leaf - me + m, z, x))

    def transposed_pairs(k, h):
        exact, pair, land, sums = r[f"exact{k}"], r["pair"], r[f"lr{k}"], r["pairsum"]
        total = None
        for d in y_order:
            m = lax.rem(leaf + 2 * d, nleaf)
            wait(pair.at[h, d], r["pr"].at[h, d])
            total = exact[h, m] + pair[h, d].astype(F32)
            if d:
                sums[h, d] = total.astype(BF)
                send(sums.at[h, d], land.at[h, d - 1], r["ls"].at[k, h], r["lr"].at[k, h], (m, z, x))
        return total

    def transposed_end(k, h, own):
        land = r[f"lr{k}"]
        wait(land.at[h], r["lr"].at[k, h])
        total = own
        for d in range(land.shape[1]):
            total += land[h, d].astype(F32)
        return total

    def backward(k, h, block, panel):
        spread_start(k, h, block)
        if k == 4:
            forward_sent(4, h)
        else:
            backward_sent(k + 1, h)
        yield
        spread_on(k, h)
        yield
        transposed_start(k, h, panel)
        yield
        if is_wide(k):
            own = transposed_pairs(k, h)
            yield
        else:
            own = r[f"exact{k}"][h, member(k)]
        return transposed_end(k, h, own)

    def backward_sent(k, h):
        wait(r[f"all{k}"].at[h, 0 : nz - 1, 0], r["bzs"].at[k, h])
        wait(r[f"all{k}"].at[h, :, 0 : nx - 1], r["bxs"].at[k, h])
        wait(r[f"lr{k}"].at[h], r["ls"].at[k, h])
        if is_wide(k):
            wait(r["pair"].at[h], r["ps"].at[h])

    def slots(name):
        ids = r["v_w" + name][...]
        places = ids.shape[1]
        blocks = nz * nx
        mine = jnp.broadcast_to(ids, (blocks, places)) == lax.broadcasted_iota(jnp.int32, (blocks, places), 0)
        before = lax.broadcasted_iota(jnp.int32, (places, places), 0) < lax.broadcasted_iota(jnp.int32, (places, places), 1)
        rank = jnp.where(mine, dot(one_hot(mine), one_hot(before)), -1.0)
        slot = lax.broadcasted_iota(jnp.int32, (ROWS, places), 0).astype(F32)
        for b in range(blocks):
            r["perm"][b] = one_hot(jnp.broadcast_to(rank[b : b + 1, :], (ROWS, places)) == slot)
        r["p" + name][...] = dot(r["perm"][...].reshape(blocks * ROWS, places), r["v_o" + name][...]).astype(BF)
        own = r["perm"][z * nx + x]
        targets = r["lay" + name].shape[0]
        offset = jnp.broadcast_to(r["v_f" + name][...], (targets, places))
        wanted = one_hot(offset == lax.broadcasted_iota(jnp.int32, (targets, places), 0))
        r["lay" + name][...] = dot_nt(wanted, own).astype(BF)
        r["sel" + name][...] = dot_nt(own, wanted).astype(BF)

    def to_targets(name, total):
        high = total.astype(BF)
        low = (total - high.astype(F32)).astype(BF)
        return dot(r["lay" + name][...], high) + dot(r["lay" + name][...], low)

    def transpose(name, panel):
        r["t_" + name][...] = panel[...].T

    loaded = set()

    def load(*wanted):
        for name in wanted:
            if name not in loaded:
                loads[name].wait()
                loaded.add(name)

    def solve(h):
        across = columns(h)
        first = h == 0
        total = yield from forward(0, h, r["v_rl"][:, across], r["v_i1"], lambda: load("i1"))
        solved_leafs = total.astype(BF)
        total = yield from forward(1, h, solved_leafs, r["p1"])
        carried = to_targets("1", total)
        load("rm")
        block = (r["v_rm"][:, across].astype(F32) - carried[:ROWS]).astype(BF)
        total = yield from forward(2, h, block, r["v_i2"], lambda: load("i2"))
        solved_mid = total.astype(BF)
        total = yield from forward(3, h, solved_mid, r["p2"])
        load("rr")
        block = (r["v_rr"][:, across].astype(F32) - carried[ROWS:] - to_targets("2", total)).astype(BF)
        total = yield from forward(4, h, block, r["v_i3"], lambda: load("i3"))

        total = yield from backward(4, h, total.astype(BF), r["t_i3"])
        solution_root = total.astype(BF)
        r["out_r"][:, across] = solution_root
        total = yield from backward(3, h, dot(r["sel2"][...], solution_root).astype(BF), r["t_p2"])
        total = yield from backward(2, h, (solved_mid.astype(F32) - total).astype(BF), r["t_i2"])
        solution_mid = total.astype(BF)
        r["out_m"][:, across] = solution_mid
        stacked = jnp.concatenate([solution_mid, solution_root], 0)
        total = yield from backward(1, h, dot(r["sel1"][...], stacked).astype(BF), r["t_p1"])
        total = yield from backward(0, h, (solved_leafs.astype(F32) - total).astype(BF), r["t_i1"])
        r["out_l"][:, across] = total.astype(BF)

    def prepare(number):
        if number == 0:
            load("w1", "o1", "f1")
            slots("1")
        elif number == 1:
            load("w2", "o2", "f2")
            slots("2")
        elif number == 2:
            load("i1")
            transpose("i1", r["v_i1"])
            transpose("p1", r["p1"])
            transpose("p2", r["p2"])
        elif number == 4:
            load("i2", "i3")
            transpose("i2", r["v_i2"])
            transpose("i3", r["v_i3"])

    load("rl")
    pl.semaphore_wait(barrier, nleaf + nz + nx - 3)

    chains = [solve(h) for h in range(PARTS)]
    for h, chain in enumerate(chains):
        for _ in range(LEAD * (PARTS - 1 - h)):
            next(chain)
    running = list(chains)
    number = 0
    while running:
        for chain in list(running):
            if next(chain, running) is running:
                running.remove(chain)
        prepare(number)
        number += 1

    for h in range(PARTS):
        backward_sent(0, h)


def shards(
    mesh_shape,
    rhs_leafs,
    rhs_mid,
    rhs_root,
    inv_leafs,
    inv_mid,
    inv_root,
    off_leafs,
    off_mid,
    owner_leafs,
    offset_leafs,
    owner_mid,
    offset_mid,
):
    nleaf, nz, nx = mesh_shape
    groups = (nleaf // 4, nleaf // 4, nleaf // 2, nleaf // 2, nleaf)
    width = NRHS // PARTS
    rows = nz * nx * ROWS

    def flat(panel):
        return panel.reshape(panel.shape[0], panel.shape[2])

    operands = {
        "rl": rhs_leafs,
        "rm": rhs_mid,
        "rr": rhs_root,
        "i1": flat(inv_leafs),
        "i2": flat(inv_mid),
        "i3": flat(inv_root),
        "o1": flat(off_leafs),
        "o2": flat(off_mid),
        "w1": owner_leafs.reshape(1, -1),
        "f1": offset_leafs.reshape(1, -1),
        "w2": owner_mid.reshape(1, -1),
        "f2": offset_mid.reshape(1, -1),
    }
    places = off_leafs.shape[0]
    names = ["in_" + name for name in operands] + ["out_l", "out_m", "out_r"]
    scratch = []

    def keep(name, shape, dtype=BF):
        names.append(name)
        scratch.append(pltpu.VMEM(shape, dtype))

    def semaphores(name, shape):
        names.append(name)
        scratch.append(pltpu.SemaphoreType.DMA(shape))

    for name, value in operands.items():
        keep("v_" + name, value.shape, value.dtype)
    semaphores("load", (len(operands),))
    keep("perm", (nz * nx, ROWS, places))
    for name, panel, targets in (("1", operands["o1"], 2 * ROWS), ("2", operands["o2"], ROWS)):
        keep("p" + name, (rows, panel.shape[1]))
        keep("t_p" + name, (panel.shape[1], rows))
        keep("lay" + name, (targets, ROWS))
        keep("sel" + name, (ROWS, targets))
    for name in ("i1", "i2", "i3"):
        keep("t_" + name, operands[name].shape[::-1])
    for k, count in enumerate(groups):
        keep(f"gat{k}", (PARTS, count, ROWS, width))
        keep(f"prod{k}", (PARTS, nx, nz, ROWS, width))
        keep(f"rx{k}", (PARTS, nx - 1, nz, ROWS, width))
        keep(f"sum{k}", (PARTS, nz, ROWS, width))
        keep(f"rz{k}", (PARTS, nz - 1, ROWS, width))
        keep(f"all{k}", (PARTS, nz, nx, ROWS, width))
        keep(f"part{k}", (PARTS, count, ROWS, width))
        keep(f"exact{k}", (PARTS, count, ROWS, width), F32)
        keep(f"lr{k}", (PARTS, (count // 2 if count == nleaf else count) - 1, ROWS, width))
    keep("pair", (PARTS, nleaf // 2, ROWS, width))
    keep("pairsum", (PARTS, nleaf // 2, ROWS, width))
    semaphores("gyr", (PARTS, nleaf // 2 - 1))
    semaphores("ps", (PARTS,))
    semaphores("pr", (PARTS, nleaf // 2))
    for name in ("gs", "gr", "xs", "zs", "zr", "bzs", "bxs", "bxr", "ls", "lr"):
        semaphores(name, (5, PARTS))
    semaphores("xr", (5, PARTS, nz // CHUNK))
    semaphores("bzr", (5, PARTS, nz - 1))

    block = jax.ShapeDtypeStruct(rhs_leafs.shape, rhs_leafs.dtype)
    return pl.pallas_call(
        functools.partial(kernel, (tuple(names), groups, nz, nx)),
        out_shape=(block, block, block),
        in_specs=[pl.BlockSpec(memory_space=pl.ANY)] * len(operands),
        out_specs=[pl.BlockSpec(memory_space=pltpu.VMEM)] * 3,
        scratch_shapes=scratch,
        compiler_params=pltpu.CompilerParams(collective_id=0, has_side_effects=True, vmem_limit_bytes=63 * 2**20),
        cost_estimate=pl.CostEstimate(flops=1_200_000_000, bytes_accessed=2_400_000, transcendentals=0),
        name="triangular_solve",
    )(*operands.values())


def solution(mesh):
    vector = P(("leaf", "row", "col"), None)
    panel = P("leaf", ("row", "col"), None)
    return jax.shard_map(
        functools.partial(shards, (mesh.shape["leaf"], mesh.shape["row"], mesh.shape["col"])),
        mesh=mesh,
        in_specs=(vector,) * 3 + (panel,) * 5 + (P("leaf", None), P("leaf")) * 2,
        out_specs=(vector,) * 3,
        check_vma=False,
    )
```

```python
import functools

import jax
import jax.numpy as jnp
from jax import lax
from jax.experimental import pallas as pl
from jax.experimental.pallas import tpu as pltpu
from jax.sharding import PartitionSpec as P

MESH = pl.DeviceIdType.MESH
BF = jnp.bfloat16
F32 = jnp.float32
ROWS = 32
NRHS = 256
PARTS = 2
CHUNK = 2
Y_FAR = 3
LEAD = 1


def z_order(nz):
    order = []
    for near in range(nz // 2, 0, -1):
        order.append(near)
        if nz - near != near:
            order.append(nz - near)
    return order + [0]


def dot(a, b):
    return jnp.dot(a, b, preferred_element_type=F32)


def dot_nt(a, b):
    return lax.dot_general(a, b, (((1,), (1,)), ((), ())), preferred_element_type=F32)


def one_hot(condition):
    return jnp.where(condition, 1.0, 0.0).astype(BF)


def kernel(sizes, *refs):
    names, groups, nz, nx = sizes
    r = dict(zip(names, refs, strict=True))
    width = NRHS // PARTS
    leaf, z, x = lax.axis_index("leaf"), lax.axis_index("row"), lax.axis_index("col")
    order = z_order(nz)
    rows = nz * nx * ROWS
    nleaf = groups[4]
    y_order = z_order(nleaf // 2)
    y_far = y_order[:Y_FAR]
    x_order = z_order(nx)[:-1]
    sibling = leaf + 1 - 2 * lax.rem(leaf, 2)

    barrier = pltpu.get_barrier_semaphore()
    for d in z_order(nz)[:-1]:
        pl.semaphore_signal(barrier, inc=1, device_id=(leaf, lax.rem(z + d, nz), x), device_id_type=MESH)
    for d in y_order[:-1]:
        for core in range(2):
            there = lax.rem(leaf - lax.rem(leaf, 2) + 2 * d + core, nleaf)
            pl.semaphore_signal(barrier, inc=1, device_id=(there, z, x), device_id_type=MESH)
    for d in range(1, nx):
        pl.semaphore_signal(barrier, inc=1, device_id=(leaf, z, lax.rem(x + d, nx)), device_id_type=MESH)
    pl.semaphore_signal(barrier, inc=1, device_id=(sibling, z, x), device_id_type=MESH)

    loads = {}
    for number, name in enumerate(("rl", "i1", "w1", "o1", "f1", "rm", "i2", "rr", "w2", "o2", "f2", "i3")):
        loads[name] = pltpu.make_async_copy(r["in_" + name], r["v_" + name], r["load"].at[number])
        loads[name].start()

    def send(source, target, send_sem, recv_sem, where):
        pltpu.make_async_remote_copy(
            src_ref=source, dst_ref=target, send_sem=send_sem, recv_sem=recv_sem, device_id=where, device_id_type=MESH
        ).start()

    def wait(ref, sem):
        pltpu.make_async_copy(ref, ref, sem).wait()

    def member(k):
        return lax.rem(leaf, groups[k])

    def columns(h):
        return slice(h * width, (h + 1) * width)

    def flipped(me, bits):
        there, bit = me, 1
        while bit <= bits:
            if bits & bit:
                there = there + bit * (1 - 2 * lax.rem(me // bit, 2))
            bit *= 2
        return there

    def flips(count):
        return sorted(range(1, count), reverse=True)

    def is_wide(k):
        return groups[k] == nleaf

    def gather_start(k, h, block):
        count, me, buf = groups[k], member(k), r[f"gat{k}"]
        buf[h, me] = block
        if is_wide(k):
            own = buf.at[h, me]
            for d in y_order[:-1]:
                send(own, own, r["gs"].at[k, h], r["gyr"].at[h, d - 1], (lax.rem(leaf + 2 * d, nleaf), z, x))
                if d in y_far:
                    send(own, own, r["gs"].at[k, h], r["gr"].at[k, h], (lax.rem(sibling + 2 * d, nleaf), z, x))
            send(own, own, r["gs"].at[k, h], r["gr"].at[k, h], (sibling, z, x))
            return
        for d in flips(count):
            send(buf.at[h, me], buf.at[h, me], r["gs"].at[k, h], r["gr"].at[k, h], (leaf - me + flipped(me, d), z, x))

    def gather_wait(k, h):
        count, buf = groups[k], r[f"gat{k}"]
        if is_wide(k):
            for d in reversed(y_order[:-1]):
                m = lax.rem(leaf + nleaf - 2 * d, nleaf)
                wait(buf.at[h, m], r["gyr"].at[h, d - 1])
                if d not in y_far:
                    send(buf.at[h, m], buf.at[h, m], r["gs"].at[k, h], r["gr"].at[k, h], (sibling, z, x))
            wait(buf.at[h, 0 : nleaf // 2], r["gr"].at[k, h])
        else:
            wait(buf.at[h, 0 : count - 1], r["gr"].at[k, h])

    def multiply_start(k, h, panel):
        count, buf, prod, land = groups[k], r[f"gat{k}"], r[f"prod{k}"], r[f"rx{k}"]
        vector = buf[h].reshape(count * ROWS, width)
        for pos, j in enumerate(order):
            there = lax.rem(z + j, nz)
            first = pl.multiple_of(there * (nx * ROWS), nx * ROWS)
            block = dot(panel[pl.ds(first, nx * ROWS), :], vector).astype(BF)
            for c in range(nx):
                prod[h, c, pos] = block[c * ROWS : (c + 1) * ROWS]
            if (pos + 1) % CHUNK == 0:
                cut = pl.ds(pos + 1 - CHUNK, CHUNK)
                for d in x_order:
                    c = lax.rem(x + d, nx)
                    send(prod.at[h, c, cut], land.at[h, d - 1, cut], r["xs"].at[k, h], r["xr"].at[k, h, pos // CHUNK], (leaf, z, c))

    def reduce_x(k, h):
        prod, land, sums, final = r[f"prod{k}"], r[f"rx{k}"], r[f"sum{k}"], r[f"rz{k}"]
        own = None
        for pos, j in enumerate(order):
            if pos % CHUNK == 0:
                cut = pl.ds(pos, CHUNK)
                wait(land.at[h, :, cut], r["xr"].at[k, h, pos // CHUNK])
            total = prod[h, x, pos].astype(F32)
            for d in range(1, nx):
                total += land[h, d - 1, pos].astype(F32)
            if j == 0:
                own = total
            else:
                sums[h, pos] = total.astype(BF)
                send(sums.at[h, pos], final.at[h, j - 1], r["zs"].at[k, h], r["zr"].at[k, h], (leaf, lax.rem(z + j, nz), x))
        return own

    def reduce_z(k, h, own):
        final = r[f"rz{k}"]
        wait(final.at[h], r["zr"].at[k, h])
        total = own
        for j in range(1, nz):
            total += final[h, j - 1].astype(F32)
        return total

    def forward(k, h, block, panel, ready=None):
        gather_start(k, h, block)
        if k:
            forward_sent(k - 1, h)
        yield
        gather_wait(k, h)
        if ready is not None:
            ready()
        multiply_start(k, h, panel)
        yield
        own = reduce_x(k, h)
        yield
        return reduce_z(k, h, own)

    def forward_sent(k, h):
        wait(r[f"gat{k}"].at[h, 0 : groups[k] - 1], r["gs"].at[k, h])
        wait(r[f"rx{k}"].at[h], r["xs"].at[k, h])
        wait(r[f"rz{k}"].at[h], r["zs"].at[k, h])

    def spread_x(k, h, row):
        buf = r[f"all{k}"]
        for d in x_order:
            send(buf.at[h, row, x], buf.at[h, row, x], r["bxs"].at[k, h], r["bxr"].at[k, h], (leaf, z, lax.rem(x + d, nx)))

    def spread_start(k, h, block):
        buf = r[f"all{k}"]
        buf[h, z, x] = block
        for j in order[:-1]:
            send(buf.at[h, z, x], buf.at[h, z, x], r["bzs"].at[k, h], r["bzr"].at[k, h, j - 1], (leaf, lax.rem(z + j, nz), x))
        spread_x(k, h, z)

    def spread_on(k, h):
        buf = r[f"all{k}"]
        for j in reversed(order[:-1]):
            row = lax.rem(z + nz - j, nz)
            wait(buf.at[h, row, x], r["bzr"].at[k, h, j - 1])
            spread_x(k, h, row)

    def transposed_start(k, h, panel):
        buf, part, exact, land, count, me = r[f"all{k}"], r[f"part{k}"], r[f"exact{k}"], r[f"lr{k}"], groups[k], member(k)
        wait(buf.at[h, :, 0 : nx - 1], r["bxr"].at[k, h])
        result = dot(panel[...], buf[h].reshape(rows, width)).reshape(count, ROWS, width)
        exact[h] = result
        part[h] = result.astype(BF)
        if is_wide(k):
            for d in y_order:
                m = lax.rem(sibling + 2 * d, nleaf)
                send(part.at[h, m], r["pair"].at[h, d], r["ps"].at[h], r["pr"].at[h, d], (sibling, z, x))
            return
        for d in flips(count):
            m = flipped(me, d)
            send(part.at[h, m], land.at[h, d - 1], r["ls"].at[k, h], r["lr"].at[k, h], (leaf - me + m, z, x))

    def transposed_pairs(k, h):
        exact, pair, land, sums = r[f"exact{k}"], r["pair"], r[f"lr{k}"], r["pairsum"]
        total = None
        for d in y_order:
            m = lax.rem(leaf + 2 * d, nleaf)
            wait(pair.at[h, d], r["pr"].at[h, d])
            total = exact[h, m] + pair[h, d].astype(F32)
            if d:
                sums[h, d] = total.astype(BF)
                send(sums.at[h, d], land.at[h, d - 1], r["ls"].at[k, h], r["lr"].at[k, h], (m, z, x))
        return total

    def transposed_end(k, h, own):
        land = r[f"lr{k}"]
        wait(land.at[h], r["lr"].at[k, h])
        total = own
        for d in range(land.shape[1]):
            total += land[h, d].astype(F32)
        return total

    def backward(k, h, block, panel):
        spread_start(k, h, block)
        if k == 4:
            forward_sent(4, h)
        else:
            backward_sent(k + 1, h)
        yield
        spread_on(k, h)
        yield
        transposed_start(k, h, panel)
        yield
        if is_wide(k):
            own = transposed_pairs(k, h)
            yield
        else:
            own = r[f"exact{k}"][h, member(k)]
        return transposed_end(k, h, own)

    def backward_sent(k, h):
        wait(r[f"all{k}"].at[h, 0 : nz - 1, 0], r["bzs"].at[k, h])
        wait(r[f"all{k}"].at[h, :, 0 : nx - 1], r["bxs"].at[k, h])
        wait(r[f"lr{k}"].at[h], r["ls"].at[k, h])
        if is_wide(k):
            wait(r["pair"].at[h], r["ps"].at[h])

    def slots(name):
        ids = r["v_w" + name][...]
        places = ids.shape[1]
        blocks = nz * nx
        mine = jnp.broadcast_to(ids, (blocks, places)) == lax.broadcasted_iota(jnp.int32, (blocks, places), 0)
        before = lax.broadcasted_iota(jnp.int32, (places, places), 0) < lax.broadcasted_iota(jnp.int32, (places, places), 1)
        rank = jnp.where(mine, dot(one_hot(mine), one_hot(before)), -1.0)
        slot = lax.broadcasted_iota(jnp.int32, (ROWS, places), 0).astype(F32)
        for b in range(blocks):
            r["perm"][b] = one_hot(jnp.broadcast_to(rank[b : b + 1, :], (ROWS, places)) == slot)
        r["p" + name][...] = dot(r["perm"][...].reshape(blocks * ROWS, places), r["v_o" + name][...]).astype(BF)
        own = r["perm"][z * nx + x]
        targets = r["lay" + name].shape[0]
        offset = jnp.broadcast_to(r["v_f" + name][...], (targets, places))
        wanted = one_hot(offset == lax.broadcasted_iota(jnp.int32, (targets, places), 0))
        r["lay" + name][...] = dot_nt(wanted, own).astype(BF)
        r["sel" + name][...] = dot_nt(own, wanted).astype(BF)

    def to_targets(name, total):
        high = total.astype(BF)
        low = (total - high.astype(F32)).astype(BF)
        return dot(r["lay" + name][...], high) + dot(r["lay" + name][...], low)

    def transpose(name, panel):
        r["t_" + name][...] = panel[...].T

    loaded = set()

    def load(*wanted):
        for name in wanted:
            if name not in loaded:
                loads[name].wait()
                loaded.add(name)

    def solve(h):
        across = columns(h)
        first = h == 0
        total = yield from forward(0, h, r["v_rl"][:, across], r["v_i1"], lambda: load("i1"))
        solved_leafs = total.astype(BF)
        total = yield from forward(1, h, solved_leafs, r["p1"])
        carried = to_targets("1", total)
        load("rm")
        block = (r["v_rm"][:, across].astype(F32) - carried[:ROWS]).astype(BF)
        total = yield from forward(2, h, block, r["v_i2"], lambda: load("i2"))
        solved_mid = total.astype(BF)
        total = yield from forward(3, h, solved_mid, r["p2"])
        load("rr")
        block = (r["v_rr"][:, across].astype(F32) - carried[ROWS:] - to_targets("2", total)).astype(BF)
        total = yield from forward(4, h, block, r["v_i3"], lambda: load("i3"))

        total = yield from backward(4, h, total.astype(BF), r["t_i3"])
        solution_root = total.astype(BF)
        r["out"][2, :, across] = solution_root
        total = yield from backward(3, h, dot(r["sel2"][...], solution_root).astype(BF), r["t_p2"])
        total = yield from backward(2, h, (solved_mid.astype(F32) - total).astype(BF), r["t_i2"])
        solution_mid = total.astype(BF)
        r["out"][1, :, across] = solution_mid
        stacked = jnp.concatenate([solution_mid, solution_root], 0)
        total = yield from backward(1, h, dot(r["sel1"][...], stacked).astype(BF), r["t_p1"])
        total = yield from backward(0, h, (solved_leafs.astype(F32) - total).astype(BF), r["t_i1"])
        r["out"][0, :, across] = total.astype(BF)

    def prepare(number):
        if number == 0:
            load("w1", "o1", "f1")
            slots("1")
        elif number == 1:
            load("w2", "o2", "f2")
            slots("2")
        elif number == 2:
            load("i1")
            transpose("i1", r["v_i1"])
            transpose("p1", r["p1"])
            transpose("p2", r["p2"])
        elif number == 4:
            load("i2", "i3")
            transpose("i2", r["v_i2"])
            transpose("i3", r["v_i3"])

    load("rl")
    pl.semaphore_wait(barrier, nleaf + nz + nx - 3)

    chains = [solve(h) for h in range(PARTS)]
    for h, chain in enumerate(chains):
        for _ in range(LEAD * (PARTS - 1 - h)):
            next(chain)
    running = list(chains)
    number = 0
    while running:
        for chain in list(running):
            if next(chain, running) is running:
                running.remove(chain)
        prepare(number)
        number += 1

    for h in range(PARTS):
        backward_sent(0, h)


def shards(
    mesh_shape,
    rhs_leafs,
    rhs_mid,
    rhs_root,
    inv_leafs,
    inv_mid,
    inv_root,
    off_leafs,
    off_mid,
    owner_leafs,
    offset_leafs,
    owner_mid,
    offset_mid,
):
    nleaf, nz, nx = mesh_shape
    groups = (nleaf // 4, nleaf // 4, nleaf // 2, nleaf // 2, nleaf)
    width = NRHS // PARTS
    rows = nz * nx * ROWS

    def flat(panel):
        return panel.reshape(panel.shape[0], panel.shape[2])

    operands = {
        "rl": rhs_leafs,
        "rm": rhs_mid,
        "rr": rhs_root,
        "i1": flat(inv_leafs),
        "i2": flat(inv_mid),
        "i3": flat(inv_root),
        "o1": flat(off_leafs),
        "o2": flat(off_mid),
        "w1": owner_leafs.reshape(1, -1),
        "f1": offset_leafs.reshape(1, -1),
        "w2": owner_mid.reshape(1, -1),
        "f2": offset_mid.reshape(1, -1),
    }
    places = off_leafs.shape[0]
    names = ["in_" + name for name in operands] + ["out"]
    scratch = []

    def keep(name, shape, dtype=BF):
        names.append(name)
        scratch.append(pltpu.VMEM(shape, dtype))

    def semaphores(name, shape):
        names.append(name)
        scratch.append(pltpu.SemaphoreType.DMA(shape))

    for name, value in operands.items():
        keep("v_" + name, value.shape, value.dtype)
    semaphores("load", (len(operands),))
    keep("perm", (nz * nx, ROWS, places))
    for name, panel, targets in (("1", operands["o1"], 2 * ROWS), ("2", operands["o2"], ROWS)):
        keep("p" + name, (rows, panel.shape[1]))
        keep("t_p" + name, (panel.shape[1], rows))
        keep("lay" + name, (targets, ROWS))
        keep("sel" + name, (ROWS, targets))
    for name in ("i1", "i2", "i3"):
        keep("t_" + name, operands[name].shape[::-1])
    for k, count in enumerate(groups):
        keep(f"gat{k}", (PARTS, count, ROWS, width))
        keep(f"prod{k}", (PARTS, nx, nz, ROWS, width))
        keep(f"rx{k}", (PARTS, nx - 1, nz, ROWS, width))
        keep(f"sum{k}", (PARTS, nz, ROWS, width))
        keep(f"rz{k}", (PARTS, nz - 1, ROWS, width))
        keep(f"all{k}", (PARTS, nz, nx, ROWS, width))
        keep(f"part{k}", (PARTS, count, ROWS, width))
        keep(f"exact{k}", (PARTS, count, ROWS, width), F32)
        keep(f"lr{k}", (PARTS, (count // 2 if count == nleaf else count) - 1, ROWS, width))
    keep("pair", (PARTS, nleaf // 2, ROWS, width))
    keep("pairsum", (PARTS, nleaf // 2, ROWS, width))
    semaphores("gyr", (PARTS, nleaf // 2 - 1))
    semaphores("ps", (PARTS,))
    semaphores("pr", (PARTS, nleaf // 2))
    for name in ("gs", "gr", "xs", "zs", "zr", "bzs", "bxs", "bxr", "ls", "lr"):
        semaphores(name, (5, PARTS))
    semaphores("xr", (5, PARTS, nz // CHUNK))
    semaphores("bzr", (5, PARTS, nz - 1))

    block = jax.ShapeDtypeStruct((3, *rhs_leafs.shape), BF)
    solved = pl.pallas_call(
        functools.partial(kernel, (tuple(names), groups, nz, nx)),
        out_shape=block,
        in_specs=[pl.BlockSpec(memory_space=pl.ANY)] * len(operands),
        out_specs=pl.BlockSpec(memory_space=pltpu.VMEM),
        scratch_shapes=scratch,
        compiler_params=pltpu.CompilerParams(collective_id=0, has_side_effects=True, vmem_limit_bytes=63 * 2**20),
        cost_estimate=pl.CostEstimate(flops=1_200_000_000, bytes_accessed=2_400_000, transcendentals=0),
        name="triangular_solve",
    )(*operands.values())
    return tuple(solved[level].astype(BF) for level in range(3))


def solution(mesh):
    vector = P(("leaf", "row", "col"), None)
    panel = P("leaf", ("row", "col"), None)
    return jax.shard_map(
        functools.partial(shards, (mesh.shape["leaf"], mesh.shape["row"], mesh.shape["col"])),
        mesh=mesh,
        in_specs=(vector,) * 3 + (panel,) * 5 + (P("leaf", None), P("leaf")) * 2,
        out_specs=(vector,) * 3,
        check_vma=False,
    )
```
